256 devices in a mesh: member: 32 (over z, y), region: 8 (over x, core).
Axes of the slice: x: 4, y: 4, z: 8, core: 2. Of those that a mesh axis runs over, the one named last changes fastest.
Arguments:
- background_realizations: float32 [1024, 262144], P('member', 'region'), may hold values from -6 to 6
- realization_expected_data: float32 [1024, 32768], P('member', 'region'), may hold values from -6 to 6
- departure_values: float32 [1024, 32768], P('member', 'region'), may hold values from -6 to 6
- instrument_dispersion: float32 [32768], P('region'), may hold values from 0.5 to 2
- window_piece_offsets: int32 [8, 33], P('region'), may hold values from 0 to 256, as said below
- window_data_pieces: int32 [8, 32, 4], P('region'), may hold values from 0 to 39, as said below
- neighbor_piece_ids: int32 [8, 2, 4], P('region'), may hold values from 0 to 31, as said below
- coupling_indicator: int32 [8, 256, 4], P('region'), may hold values 0 or 1
Outputs:
- analysis: float32 [1024, 262144], P('member', 'region')
The draws below stay inside these ranges and needn't reach their ends.
Inputs may be any that keep to these rules, and one draw needn't show every extreme that they name: `window_piece_offsets`: each row starts at 0, ends at 256 and rises by 1 or more at each entry; entry p lies within 3 of p * 8; in every row one patch spans exactly 14 blocks. `window_data_pieces`: entries index a region's extended observation blocks: 0 to 31 its own, then 4 received from the region before it, then 4 from the region after it; the 4 entries of a patch differ. `neighbor_piece_ids`: entries index the sending region's own observation blocks; the 4 entries of a row differ.
All inputs are finite; a program needn't handle non-finite values. No bound on the sum of `coupling_indicator` on one device may be relied on, other than what follows from the above.
Results may differ from the reference program's by a relative error of at most 0.0003.
Values sent between devices are 32-bit elements; how exact they have to be, the bound alone decides.
No kernel may reach another device: no remote copies, remote signals or barrier semaphores. Data moves between devices by JAX's collectives and lax.ppermute only.
A program may use at most 128 MiB of HBM per device.

```python
import math
import jax
import jax.numpy as jnp
from jax import lax

REALIZATION_NUM = 1024
PIECE_LENGTH = 128
OBS_PER = 4
LOCAL = 512
BLK_DEV = 8
HALF = 3
SEGMENTS_AREA = 256
OBSERVED_PARTS = 32
HB = 4
EXT = 40
DOMAIN_NUMBER = 8
PATCHES = 32
N_REGION = 8


def distinct_rows(key, shape_lead, choices, keep):
    scores = jax.random.randint(key, shape_lead + (choices,), 0, 2 ** 20) * choices
    scores = scores + jnp.arange(choices).astype(jnp.int32)
    order = jnp.argsort(scores, axis=-1, stable=True)
    return order[..., :keep].astype(jnp.int32)


def draw_window_piece_offsets(key, part):
    first_key, second_key = jax.random.split(jax.random.fold_in(key, 11))
    offsets = jax.random.randint(first_key, (DOMAIN_NUMBER, PATCHES + 1), -HALF, HALF + 1)
    chosen_patch = jax.random.randint(second_key, (DOMAIN_NUMBER, 1), 1, PATCHES - 1)
    column = jnp.arange(PATCHES + 1)[None, :]
    offsets = jnp.where(column == chosen_patch, -HALF, offsets)
    offsets = jnp.where(column == chosen_patch + 1, HALF, offsets)
    offsets = jnp.where((column == 0) | (column == PATCHES), 0, offsets)
    return (column * BLK_DEV + offsets).astype(jnp.int32)


def draw_window_data_pieces(key, part):
    return distinct_rows(jax.random.fold_in(key, 23), (DOMAIN_NUMBER, PATCHES), EXT, OBS_PER)


def draw_neighbor_piece_ids(key, part):
    return distinct_rows(jax.random.fold_in(key, 37), (DOMAIN_NUMBER, 2), OBSERVED_PARTS, HB)


def with_ends(drawn, key, least, top_value):
    longest = drawn.shape.index(max(drawn.shape))
    spots = []
    for shift in (0, 1):
        where = [jax.random.randint(jax.random.fold_in(key, axis), (), 0, length) for axis, length in enumerate(drawn.shape)]
        where[longest] = (where[longest] + shift) % drawn.shape[longest]
        spots.append(tuple(where))
    return drawn.at[spots[0]].set(least).at[spots[1]].set(top_value)


def levels(own_key, shape, cuts, low, top_value):
    loudness = 1.0
    for dim, blocks in cuts:
        steps = jax.random.uniform(jax.random.fold_in(jax.random.fold_in(own_key, 6), dim), (blocks,), jnp.float32, low / len(cuts), top_value / len(cuts))
        loudness = loudness * jnp.repeat(jnp.exp(steps), shape[dim] // blocks).reshape((-1,) + (1,) * (len(shape) - 1 - dim))
    return loudness


def gaussian(key, dims, width, most, cuts=(), kind=jnp.bfloat16):
    values = jax.random.normal(key, dims, jnp.float32) * width
    if len(cuts) > 0:
        values = levels(key, dims, cuts, -0.22, 0.18) * values
    return jnp.clip(values, min=-most, max=most).astype(kind)


def setup_inputs(seed: int = 0) -> dict:
    arg_keys = jax.random.split(jax.random.key(seed), 9)
    background_realizations = gaussian(arg_keys[0], (REALIZATION_NUM, DOMAIN_NUMBER * SEGMENTS_AREA * PIECE_LENGTH), 1.0, 6.0, ((0, 32), (1, 8)), jnp.float32)
    realization_expected_data = gaussian(arg_keys[1], (REALIZATION_NUM, DOMAIN_NUMBER * OBSERVED_PARTS * PIECE_LENGTH), 1.0, 6.0, ((0, 32), (1, 8)), jnp.float32)
    departure_values = gaussian(arg_keys[2], (REALIZATION_NUM, DOMAIN_NUMBER * OBSERVED_PARTS * PIECE_LENGTH), 1.0, 6.0, ((0, 32), (1, 8)), jnp.float32)
    instrument_dispersion = jnp.clip(jnp.exp(math.log(2.0) - 1.3862944 * jax.random.uniform(arg_keys[3], (DOMAIN_NUMBER * OBSERVED_PARTS * PIECE_LENGTH,), jnp.float32) ** levels(arg_keys[3], (DOMAIN_NUMBER * OBSERVED_PARTS * PIECE_LENGTH,), ((0, 8),), -0.2, 0.2)), 0.5, 2.0)
    window_piece_offsets = draw_window_piece_offsets(jax.random.fold_in(arg_keys[8], 71), 0)
    window_data_pieces = draw_window_data_pieces(jax.random.fold_in(arg_keys[8], 71), 0)
    neighbor_piece_ids = draw_neighbor_piece_ids(jax.random.fold_in(arg_keys[8], 71), 0)
    coupling_indicator = with_ends((jax.random.randint(arg_keys[7], (DOMAIN_NUMBER, SEGMENTS_AREA, OBS_PER), 0, 4) < 3).astype(jnp.int32), jax.random.fold_in(arg_keys[7], 1), 0, 1)
    return dict(background_realizations=background_realizations, realization_expected_data=realization_expected_data, departure_values=departure_values, instrument_dispersion=instrument_dispersion, window_piece_offsets=window_piece_offsets, window_data_pieces=window_data_pieces, neighbor_piece_ids=neighbor_piece_ids, coupling_indicator=coupling_indicator)


highest = lax.Precision.HIGHEST

def listed(stack, lists, axis_at):
    return jax.vmap(lambda region_data, region_list: jnp.take(region_data, region_list, axis=axis_at))(stack, lists)

def extended(stack, neighbor_piece_ids, axis_at):
    before = jnp.roll(listed(stack, neighbor_piece_ids[:, 0], axis_at), 1, axis=0)
    after = jnp.roll(listed(stack, neighbor_piece_ids[:, 1], axis_at), -1, axis=0)
    return jnp.concatenate([stack, before, after], axis=axis_at + 1)

def reference(background_realizations, realization_expected_data, departure_values, instrument_dispersion, window_piece_offsets, window_data_pieces, neighbor_piece_ids, coupling_indicator):
    realization_records = REALIZATION_NUM
    domain_records = N_REGION
    sample_vectors = background_realizations.reshape(realization_records, domain_records, SEGMENTS_AREA, PIECE_LENGTH).transpose(1, 0, 2, 3)
    expected_data = realization_expected_data.reshape(realization_records, domain_records, OBSERVED_PARTS, PIECE_LENGTH).transpose(1, 0, 2, 3)
    innovated = departure_values.reshape(realization_records, domain_records, OBSERVED_PARTS, PIECE_LENGTH).transpose(1, 0, 2, 3)
    variance = instrument_dispersion.reshape(domain_records, OBSERVED_PARTS, PIECE_LENGTH)
    pred_ext = extended(expected_data, neighbor_piece_ids, 1)
    innov_ext = extended(innovated, neighbor_piece_ids, 1)
    var_ext = extended(variance, neighbor_piece_ids, 0)

    def one_region(inputs):
        states, pred_region, innov_region, var_region, bounds_row, lists_row, cover_rows = inputs
        centred = states - jnp.mean(states, axis=0, keepdims=True)

        def solve_patch(chosen):
            raw = jnp.take(pred_region, chosen, axis=1).reshape(realization_records, LOCAL)
            perturbed = raw - jnp.mean(raw, axis=0, keepdims=True)
            local_innov = jnp.take(innov_region, chosen, axis=1).reshape(realization_records, LOCAL)
            local_var = jnp.take(var_region, chosen, axis=0).reshape(LOCAL)
            cov_obs = jnp.dot(perturbed.T.astype(jnp.float32), perturbed.astype(jnp.float32), precision=highest, preferred_element_type=jnp.float32) / (realization_records - 1.0)
            cov_obs = cov_obs + jnp.diag(local_var)
            factor = jnp.linalg.cholesky(cov_obs)
            weights = jax.scipy.linalg.cho_solve((factor, True), local_innov.T)
            return (perturbed, weights)
        perts, weights_all = lax.map(solve_patch, lists_row)
        block_ids = jnp.arange(SEGMENTS_AREA).astype(jnp.int32)
        owners = jnp.sum((bounds_row[None, 1:-1] <= block_ids[:, None]).astype(jnp.int32), axis=1)

        def one_block(block_inputs):
            column, owner_id, mark_row = block_inputs
            perturbed = perts[owner_id]
            weights = weights_all[owner_id]
            kalman_gain = jnp.dot(column.T.astype(jnp.float32), perturbed.astype(jnp.float32), precision=highest, preferred_element_type=jnp.float32) / (realization_records - 1.0)
            kalman_gain = kalman_gain * jnp.repeat(mark_row.astype(jnp.float32), PIECE_LENGTH)[None, :]
            return jnp.dot(weights.T.astype(jnp.float32), kalman_gain.T.astype(jnp.float32), precision=highest, preferred_element_type=jnp.float32)
        increments = lax.map(one_block, (centred.transpose(1, 0, 2), owners, cover_rows))
        return states + increments.transpose(1, 0, 2)
    analysed = lax.map(one_region, (sample_vectors, pred_ext, innov_ext, var_ext, window_piece_offsets, window_data_pieces, coupling_indicator))
    return analysed.transpose(1, 0, 2, 3).reshape(realization_records, domain_records * SEGMENTS_AREA * PIECE_LENGTH)
```

```python
import jax
import jax.numpy as jnp
from jax import lax
from jax.experimental import pallas as pl
from jax.experimental.pallas import tpu as pltpu
from jax.sharding import PartitionSpec as P

PIECE = 128
OBS_PER = 4
LOCAL = 512
HALF = 3
ROWS, COLS = 8, 4
BOTH = ("member", "region")

highest = lax.Precision.HIGHEST
f32 = jnp.float32
in_vmem = pl.BlockSpec(memory_space=pltpu.VMEM)
in_smem = pl.BlockSpec(memory_space=pltpu.SMEM)


def dot(a, b, da, db):
    return lax.dot_general(
        a, b, (((da,), (db,)), ((), ())), precision=highest, preferred_element_type=f32
    )


def column_of(z, r, core):
    return ((r if z % 2 == 0 else COLS - 1 - r) + 2 * core) % COLS


def place_on_row(z, y, core):
    r = lax.rem(y + 2 * core, COLS)
    return jnp.where(lax.rem(z, 2) == 0, r, COLS - 1 - r)


def along_snake(x, step):
    regions = lax.axis_size("region")
    total = ROWS * COLS
    route = []
    for g in range(regions):
        spot = [z * COLS + column_of(z, r, g % 2) for z in range(ROWS) for r in range(COLS)]
        for p in range(total):
            if 0 <= p + step < total:
                route.append((spot[p] * regions + g, spot[p + step] * regions + g))
    return lax.ppermute(x, BOTH, route)


def exchange(x):
    return lax.all_to_all(x, "member", split_axis=0, concat_axis=0, tiled=True)


def states_kernel(core_ref, x_ref, rim_ref, mid_ref):
    z = pl.program_id(0)
    for y in range(COLS):
        base = place_on_row(z, y, core_ref[0]) * 1024
        rim_ref[y, :, :384] = x_ref[:, pl.ds(pl.multiple_of(base, 128), 384)]
        mid_ref[y] = x_ref[:, pl.ds(pl.multiple_of(base + 384, 128), 256)]
        rim_ref[y, :, 384:] = x_ref[:, pl.ds(pl.multiple_of(base + 640, 128), 384)]


def lay_states(core, x):
    members = x.shape[0]
    widths = (768, 256)
    return pl.pallas_call(
        states_kernel,
        grid=(ROWS,),
        in_specs=[in_smem, pl.BlockSpec((members, 4096), lambda z: (0, z))],
        out_specs=[pl.BlockSpec((COLS, members, w), lambda z: (z, 0, 0)) for w in widths],
        out_shape=[jax.ShapeDtypeStruct((ROWS * COLS, members, w), f32) for w in widths],
        compiler_params=pltpu.CompilerParams(vmem_limit_bytes=16 * 2**20),
        cost_estimate=pl.CostEstimate(flops=0, bytes_accessed=2**23, transcendentals=0),
    )(core, x)


def halo_kernel(ids_ref, pred_ref, innov_ref, var_ref, before_ref, after_ref):
    members = pred_ref.shape[0]
    for j, out_ref in enumerate((before_ref, after_ref)):
        for k in range(4):
            at = pl.ds(pl.multiple_of(ids_ref[j, k] * PIECE, PIECE), PIECE)
            to = slice(k * PIECE, (k + 1) * PIECE)
            out_ref[:members, to] = pred_ref[:, at]
            out_ref[members : 2 * members, to] = innov_ref[:, at]
            out_ref[2 * members :, to] = jnp.broadcast_to(var_ref[:, at], (8, PIECE))


def lay_halo(ids, pred, innov, var):
    rows = 2 * pred.shape[0] + 8
    return pl.pallas_call(
        halo_kernel,
        in_specs=[in_smem, in_vmem, in_vmem, in_vmem],
        out_specs=[in_vmem, in_vmem],
        out_shape=[jax.ShapeDtypeStruct((rows, LOCAL), f32)] * 2,
        compiler_params=pltpu.CompilerParams(vmem_limit_bytes=8 * 2**20),
        cost_estimate=pl.CostEstimate(flops=0, bytes_accessed=2**20, transcendentals=0),
    )(ids, pred, innov, var)


def obs_kernel(
    place_ref, lists_ref, pred_ref, innov_ref, var_ref, before_ref, after_ref,
    pred_out, innov_out, var_out, pred_ext, innov_ext, var_ext,
):
    members, own = pred_ref.shape
    for ext, ref, lo, hi in (
        (pred_ext, pred_ref, 0, members),
        (innov_ext, innov_ref, members, 2 * members),
    ):
        ext[:, :own] = ref[...]
        ext[:, own : own + LOCAL] = before_ref[lo:hi, :]
        ext[:, own + LOCAL :] = after_ref[lo:hi, :]
    var_ext[:, :own] = jnp.broadcast_to(var_ref[...], (8, own))
    var_ext[:, own : own + LOCAL] = before_ref[2 * members :, :]
    var_ext[:, own + LOCAL :] = after_ref[2 * members :, :]
    core, mine = place_ref[0], place_ref[1]

    def one(i, carry):
        z, y = i // COLS, lax.rem(i, COLS)
        patch = z * COLS + place_on_row(z, y, core)
        for k in range(OBS_PER):
            at = pl.ds(pl.multiple_of(lists_ref[patch, k] * PIECE, PIECE), PIECE)
            to = slice(k * PIECE, (k + 1) * PIECE)
            pred_out[i, :, to] = pred_ext[:, at]
            innov_out[i, :, to] = innov_ext[:, at]
        return carry

    lax.fori_loop(0, ROWS * COLS, one, 0)
    for k in range(OBS_PER):
        at = pl.ds(pl.multiple_of(lists_ref[mine, k] * PIECE, PIECE), PIECE)
        var_out[:, k * PIECE : (k + 1) * PIECE] = var_ext[:, at]


def lay_obs(place, lists, pred, innov, var, before, after):
    members, own = pred.shape
    sent = jax.ShapeDtypeStruct((ROWS * COLS, members, LOCAL), f32)
    return pl.pallas_call(
        obs_kernel,
        in_specs=[in_smem, in_smem] + [in_vmem] * 5,
        out_specs=[in_vmem] * 3,
        out_shape=[sent, sent, jax.ShapeDtypeStruct((8, LOCAL), f32)],
        scratch_shapes=[
            pltpu.VMEM((members, own + 2 * LOCAL), f32),
            pltpu.VMEM((members, own + 2 * LOCAL), f32),
            pltpu.VMEM((8, own + 2 * LOCAL), f32),
        ],
        compiler_params=pltpu.CompilerParams(vmem_limit_bytes=24 * 2**20),
        cost_estimate=pl.CostEstimate(flops=0, bytes_accessed=6 * 2**20, transcendentals=0),
    )(place, lists, pred, innov, var, before, after)


def finish_kernel(core_ref, x_ref, mid_ref, rim_ref, out_ref):
    z = pl.program_id(0)
    for y in range(COLS):
        base = place_on_row(z, y, core_ref[0]) * 1024
        for lo, width, ref, at in ((0, 384, rim_ref, 0), (384, 256, mid_ref, 0), (640, 384, rim_ref, 384)):
            to = pl.ds(pl.multiple_of(base + lo, 128), width)
            out_ref[:, to] = x_ref[:, to] + ref[y, :, at : at + width]


def finish(core, x, mid, rim):
    members = x.shape[0]
    return pl.pallas_call(
        finish_kernel,
        grid=(ROWS,),
        in_specs=[
            in_smem,
            pl.BlockSpec((members, 4096), lambda z: (0, z)),
            pl.BlockSpec((COLS, members, 256), lambda z: (z, 0, 0)),
            pl.BlockSpec((COLS, members, 768), lambda z: (z, 0, 0)),
        ],
        out_specs=pl.BlockSpec((members, 4096), lambda z: (0, z)),
        out_shape=jax.ShapeDtypeStruct(x.shape, f32),
        compiler_params=pltpu.CompilerParams(vmem_limit_bytes=16 * 2**20),
        cost_estimate=pl.CostEstimate(flops=2**20, bytes_accessed=3 * 2**22, transcendentals=0),
    )(core, x, mid, rim)


def factor_block(a_ref, m_ref):
    n = PIECE
    row = lax.broadcasted_iota(jnp.int32, (8, n), 0)
    for lo in range(0, n, 8):
        p = a_ref[lo : lo + 8, :]
        q = m_ref[lo : lo + 8, :]
        b = [jnp.broadcast_to(p[:, lo + i : lo + i + 1], (8, n)) for i in range(8)]
        d = jnp.ones((8, n), f32)
        for i in range(8):
            pivot = jnp.broadcast_to(b[i][i : i + 1, :], (8, n))
            d = jnp.where(row == i, pivot, d)
            if i < 7:
                f = jnp.where(row > i, b[i] / pivot, 0.0)
                for j in range(i + 1, 8):
                    b[j] = b[j] - f * jnp.broadcast_to(b[j][i : i + 1, :], (8, n))
                p = p - f * jnp.broadcast_to(p[i : i + 1, :], (8, n))
                q = q - f * jnp.broadcast_to(q[i : i + 1, :], (8, n))
        s = lax.rsqrt(d)
        u = p * s
        v = q * s
        m_ref[lo : lo + 8, :] = v
        if lo + 8 < n:
            step = dot(u.T, jnp.concatenate([u, v], axis=1), 1, 0)
            a_ref[lo + 8 :, :] = a_ref[lo + 8 :, :] - step[lo + 8 :, :n]
            m_ref[lo + 8 :, :] = m_ref[lo + 8 :, :] - step[lo + 8 :, n:]


def factor_kernel(c_ref, t_ref, a_ref, d_ref, m_ref):
    n = PIECE
    a_ref[...] = c_ref[...]
    t_ref[...] = jnp.zeros((LOCAL, LOCAL), f32)
    eye = lax.broadcasted_iota(jnp.int32, (n, n), 0) == lax.broadcasted_iota(jnp.int32, (n, n), 1)
    for lo in range(0, LOCAL, n):
        hi = lo + n
        d_ref[...] = a_ref[lo:hi, lo:hi]
        m_ref[...] = eye.astype(f32)
        factor_block(d_ref, m_ref)
        m = m_ref[...]
        if lo:
            t_ref[lo:hi, :lo] = dot(m, t_ref[lo:hi, :lo], 1, 0)
        t_ref[lo:hi, lo:hi] = m
        if hi < LOCAL:
            u = dot(m, a_ref[lo:hi, hi:], 1, 0)
            a_ref[hi:, hi:] = a_ref[hi:, hi:] - dot(u, u, 0, 0)
            t_ref[hi:, :hi] = t_ref[hi:, :hi] - dot(u, t_ref[lo:hi, :hi], 0, 0)


def inverse_factor(cov):
    return pl.pallas_call(
        factor_kernel,
        in_specs=[in_vmem],
        out_specs=in_vmem,
        out_shape=jax.ShapeDtypeStruct((LOCAL, LOCAL), f32),
        scratch_shapes=[
            pltpu.VMEM((LOCAL, LOCAL), f32),
            pltpu.VMEM((PIECE, PIECE), f32),
            pltpu.VMEM((PIECE, PIECE), f32),
        ],
        compiler_params=pltpu.CompilerParams(vmem_limit_bytes=16 * 2**20),
        cost_estimate=pl.CostEstimate(flops=36 * 10**9, bytes_accessed=2**21, transcendentals=0),
    )(cov)


def in_order(*arrays):
    return lax.optimization_barrier(arrays)


def body(
    background_realizations,
    realization_expected_data,
    departure_values,
    instrument_dispersion,
    window_piece_offsets,
    window_data_pieces,
    neighbor_piece_ids,
    coupling_indicator,
):
    own_index = lax.axis_index("member")
    region = lax.axis_index("region")
    regions = lax.axis_size("region")
    members = lax.axis_size("member") * background_realizations.shape[0]
    core = lax.rem(region, 2)
    z, y = own_index // COLS, lax.rem(own_index, COLS)
    mine = z * COLS + place_on_row(z, y, core)
    core_word = core.reshape(1)

    rim_s, mid_s = lay_states(core_word, background_realizations)
    rim = exchange(rim_s)

    var = instrument_dispersion.reshape(1, -1)
    to_next, to_last = lay_halo(
        neighbor_piece_ids[0], realization_expected_data, departure_values, var
    )
    before = lax.ppermute(to_next, "region", [(i, (i + 1) % regions) for i in range(regions)])
    behind = lax.ppermute(to_last, "region", [(i, (i - 1) % regions) for i in range(regions)])
    pred_s, innov_s, var_rows = lay_obs(
        jnp.stack([core, mine]),
        window_data_pieces[0],
        realization_expected_data,
        departure_values,
        var,
        before,
        behind,
    )

    def whole(x):
        return x.reshape(members, x.shape[2])

    def in_parts(x):
        return x.reshape(lax.axis_size("member"), -1, x.shape[1])

    cover = jnp.pad(coupling_indicator[0].astype(f32), ((HALF, HALF), (0, 0)))
    cover = lax.dynamic_slice_in_dim(cover, 8 * mine, 14, 0)
    cover = jnp.broadcast_to(cover[:, :, None], (14, OBS_PER, PIECE)).reshape(14, LOCAL)
    starts = lax.dynamic_slice_in_dim(window_piece_offsets[0], mine, 2, 0) - 8 * mine
    block = lax.broadcasted_iota(jnp.int32, (1, 384), 1) // PIECE

    rim = whole(rim)
    head, tail = rim[:, :384], rim[:, 384:]
    rim, pred_s = in_order(rim, pred_s)
    pred = exchange(pred_s)
    beyond = along_snake(head, -1)
    ahead = along_snake(tail, 1)

    pred, innov_s = in_order(pred, innov_s)
    innov = exchange(innov_s)
    pred = whole(pred)
    perturbed = pred - jnp.mean(pred, axis=0, keepdims=True)
    cov = dot(perturbed, perturbed, 0, 0) / (members - 1.0)
    cov = cov + jnp.eye(LOCAL, dtype=f32) * var_rows[:1]
    root = inverse_factor(cov)

    def gain(x, lo):
        count = x.shape[1] // PIECE
        centred = x - jnp.mean(x, axis=0, keepdims=True)
        g = dot(centred, perturbed, 0, 0) / (members - 1.0)
        g = g.reshape(count, PIECE, LOCAL) * cover[lo : lo + count, None, :]
        return g.reshape(count * PIECE, LOCAL)

    root, beyond, ahead = in_order(root, beyond, ahead)
    beyond_gain = gain(beyond, 11)
    ahead_gain = gain(ahead, 0)

    innov, root, mid_s, beyond_gain, ahead_gain = in_order(innov, root, mid_s, beyond_gain, ahead_gain)
    mid = exchange(mid_s)
    weights = dot(root, dot(root, whole(innov), 1, 1), 0, 0)
    beyond_inc = dot(weights, beyond_gain, 0, 1)
    ahead_inc = dot(weights, ahead_gain, 0, 1)
    head_back = along_snake(beyond_inc, 1)
    tail_back = along_snake(ahead_inc, -1)
    mid, beyond_inc, ahead_inc = in_order(mid, beyond_inc, ahead_inc)
    mid_inc = dot(weights, gain(whole(mid), 6), 0, 1)
    mid_out = exchange(in_parts(mid_inc))
    mid_inc, late_weights, head, tail = in_order(mid_inc, weights, head, tail)
    head_own = dot(late_weights, gain(head, 3), 0, 1)
    tail_own = dot(late_weights, gain(tail, 8), 0, 1)
    head_own, tail_own, head_back, tail_back = in_order(head_own, tail_own, head_back, tail_back)
    head_inc = jnp.where(block < starts[0], head_back, head_own)
    tail_inc = jnp.where(block + 5 >= starts[1], tail_back, tail_own)
    rim_inc = jnp.concatenate([head_inc, tail_inc], axis=1)
    mid_out, rim_inc = in_order(mid_out, rim_inc)
    rim_out = exchange(in_parts(rim_inc))
    return finish(core_word, background_realizations, mid_out, rim_out)


def solution(mesh):
    return jax.shard_map(
        body,
        mesh=mesh,
        in_specs=(
            P("member", "region"),
            P("member", "region"),
            P("member", "region"),
            P("region"),
            P("region", None),
            P("region", None, None),
            P("region", None, None),
            P("region", None, None),
        ),
        out_specs=P("member", "region"),
        check_vma=False,
    )
```

```python
import jax
import jax.numpy as jnp
from jax import lax
from jax.experimental import pallas as pl
from jax.experimental.pallas import tpu as pltpu
from jax.sharding import PartitionSpec as P

PIECE = 128
OBS_PER = 4
LOCAL = 512
HALF = 3
ROWS, COLS = 8, 4
BOTH = ("member", "region")

highest = lax.Precision.HIGHEST
high = lax.Precision.HIGH
f32 = jnp.float32
in_vmem = pl.BlockSpec(memory_space=pltpu.VMEM)
in_smem = pl.BlockSpec(memory_space=pltpu.SMEM)


def dot(a, b, da, db):
    return lax.dot_general(
        a, b, (((da,), (db,)), ((), ())), precision=highest, preferred_element_type=f32
    )


def column_of(z, r, core):
    return ((r if z % 2 == 0 else COLS - 1 - r) + 2 * core) % COLS


def place_on_row(z, y, core):
    r = lax.rem(y + 2 * core, COLS)
    return jnp.where(lax.rem(z, 2) == 0, r, COLS - 1 - r)


def along_snake(x, step):
    regions = lax.axis_size("region")
    total = ROWS * COLS
    route = []
    for g in range(regions):
        spot = [z * COLS + column_of(z, r, g % 2) for z in range(ROWS) for r in range(COLS)]
        for p in range(total):
            if 0 <= p + step < total:
                route.append((spot[p] * regions + g, spot[p + step] * regions + g))
    return lax.ppermute(x, BOTH, route)


def exchange(x):
    return lax.all_to_all(x, "member", split_axis=0, concat_axis=0, tiled=True)


def states_kernel(core_ref, x_ref, rim_ref, mid_ref):
    z = pl.program_id(0)
    for y in range(COLS):
        base = place_on_row(z, y, core_ref[0]) * 1024
        rim_ref[y, :, :384] = x_ref[:, pl.ds(pl.multiple_of(base, 128), 384)]
        mid_ref[y] = x_ref[:, pl.ds(pl.multiple_of(base + 384, 128), 256)]
        rim_ref[y, :, 384:] = x_ref[:, pl.ds(pl.multiple_of(base + 640, 128), 384)]


def lay_states(core, x):
    members = x.shape[0]
    widths = (768, 256)
    return pl.pallas_call(
        states_kernel,
        grid=(ROWS,),
        in_specs=[in_smem, pl.BlockSpec((members, 4096), lambda z: (0, z))],
        out_specs=[pl.BlockSpec((COLS, members, w), lambda z: (z, 0, 0)) for w in widths],
        out_shape=[jax.ShapeDtypeStruct((ROWS * COLS, members, w), f32) for w in widths],
        compiler_params=pltpu.CompilerParams(vmem_limit_bytes=16 * 2**20),
        cost_estimate=pl.CostEstimate(flops=0, bytes_accessed=2**23, transcendentals=0),
    )(core, x)


def halo_kernel(ids_ref, pred_ref, innov_ref, var_ref, before_ref, after_ref):
    members = pred_ref.shape[0]
    for j, out_ref in enumerate((before_ref, after_ref)):
        for k in range(4):
            at = pl.ds(pl.multiple_of(ids_ref[j, k] * PIECE, PIECE), PIECE)
            to = slice(k * PIECE, (k + 1) * PIECE)
            out_ref[:members, to] = pred_ref[:, at]
            out_ref[members : 2 * members, to] = innov_ref[:, at]
            out_ref[2 * members :, to] = jnp.broadcast_to(var_ref[:, at], (8, PIECE))


def lay_halo(ids, pred, innov, var):
    rows = 2 * pred.shape[0] + 8
    return pl.pallas_call(
        halo_kernel,
        in_specs=[in_smem, in_vmem, in_vmem, in_vmem],
        out_specs=[in_vmem, in_vmem],
        out_shape=[jax.ShapeDtypeStruct((rows, LOCAL), f32)] * 2,
        compiler_params=pltpu.CompilerParams(vmem_limit_bytes=8 * 2**20),
        cost_estimate=pl.CostEstimate(flops=0, bytes_accessed=2**20, transcendentals=0),
    )(ids, pred, innov, var)


def obs_kernel(
    place_ref, lists_ref, pred_ref, innov_ref, var_ref, before_ref, after_ref,
    pred_out, innov_out, var_out, pred_ext, innov_ext, var_ext,
):
    members, own = pred_ref.shape
    for ext, ref, lo, hi in (
        (pred_ext, pred_ref, 0, members),
        (innov_ext, innov_ref, members, 2 * members),
    ):
        ext[:, :own] = ref[...]
        ext[:, own : own + LOCAL] = before_ref[lo:hi, :]
        ext[:, own + LOCAL :] = after_ref[lo:hi, :]
    var_ext[:, :own] = jnp.broadcast_to(var_ref[...], (8, own))
    var_ext[:, own : own + LOCAL] = before_ref[2 * members :, :]
    var_ext[:, own + LOCAL :] = after_ref[2 * members :, :]
    core, mine = place_ref[0], place_ref[1]

    def one(i, carry):
        z, y = i // COLS, lax.rem(i, COLS)
        patch = z * COLS + place_on_row(z, y, core)
        for k in range(OBS_PER):
            at = pl.ds(pl.multiple_of(lists_ref[patch, k] * PIECE, PIECE), PIECE)
            to = slice(k * PIECE, (k + 1) * PIECE)
            pred_out[i, :, to] = pred_ext[:, at]
            innov_out[i, :, to] = innov_ext[:, at]
        return carry

    lax.fori_loop(0, ROWS * COLS, one, 0)
    for k in range(OBS_PER):
        at = pl.ds(pl.multiple_of(lists_ref[mine, k] * PIECE, PIECE), PIECE)
        var_out[:, k * PIECE : (k + 1) * PIECE] = var_ext[:, at]


def lay_obs(place, lists, pred, innov, var, before, after):
    members, own = pred.shape
    sent = jax.ShapeDtypeStruct((ROWS * COLS, members, LOCAL), f32)
    return pl.pallas_call(
        obs_kernel,
        in_specs=[in_smem, in_smem] + [in_vmem] * 5,
        out_specs=[in_vmem] * 3,
        out_shape=[sent, sent, jax.ShapeDtypeStruct((8, LOCAL), f32)],
        scratch_shapes=[
            pltpu.VMEM((members, own + 2 * LOCAL), f32),
            pltpu.VMEM((members, own + 2 * LOCAL), f32),
            pltpu.VMEM((8, own + 2 * LOCAL), f32),
        ],
        compiler_params=pltpu.CompilerParams(vmem_limit_bytes=24 * 2**20),
        cost_estimate=pl.CostEstimate(flops=0, bytes_accessed=6 * 2**20, transcendentals=0),
    )(place, lists, pred, innov, var, before, after)


def finish_kernel(core_ref, x_ref, mid_ref, rim_ref, out_ref):
    z = pl.program_id(0)
    for y in range(COLS):
        base = place_on_row(z, y, core_ref[0]) * 1024
        for lo, width, ref, at in ((0, 384, rim_ref, 0), (384, 256, mid_ref, 0), (640, 384, rim_ref, 384)):
            to = pl.ds(pl.multiple_of(base + lo, 128), width)
            out_ref[:, to] = x_ref[:, to] + ref[y, :, at : at + width]


def finish(core, x, mid, rim):
    members = x.shape[0]
    return pl.pallas_call(
        finish_kernel,
        grid=(ROWS,),
        in_specs=[
            in_smem,
            pl.BlockSpec((members, 4096), lambda z: (0, z)),
            pl.BlockSpec((COLS, members, 256), lambda z: (z, 0, 0)),
            pl.BlockSpec((COLS, members, 768), lambda z: (z, 0, 0)),
        ],
        out_specs=pl.BlockSpec((members, 4096), lambda z: (0, z)),
        out_shape=jax.ShapeDtypeStruct(x.shape, f32),
        compiler_params=pltpu.CompilerParams(vmem_limit_bytes=16 * 2**20),
        cost_estimate=pl.CostEstimate(flops=2**20, bytes_accessed=3 * 2**22, transcendentals=0),
    )(core, x, mid, rim)


def hold_kernel(in_ref, out_ref):
    out_ref[0] = in_ref[0]
    out_ref[1] = in_ref[1]


def hold(starts):
    return pl.pallas_call(
        hold_kernel,
        in_specs=[in_smem],
        out_specs=in_smem,
        out_shape=jax.ShapeDtypeStruct((2,), jnp.int32),
        cost_estimate=pl.CostEstimate(flops=10**11, bytes_accessed=8, transcendentals=0),
    )(starts)


def choose_kernel(starts_ref, own_ref, head_ref, tail_ref, out_ref):
    for j in range(HALF):
        at = slice(j * PIECE, (j + 1) * PIECE)
        out_ref[:, at] = jnp.where(j < starts_ref[0], head_ref[:, at], own_ref[:, at])
        to = slice((HALF + j) * PIECE, (HALF + j + 1) * PIECE)
        out_ref[:, to] = jnp.where(j + 5 >= starts_ref[1], tail_ref[:, at], own_ref[:, to])


def choose(starts, own, head, tail):
    rows = own.shape[0] // 4
    return pl.pallas_call(
        choose_kernel,
        grid=(4,),
        in_specs=[in_smem] + [pl.BlockSpec((rows, w), lambda i: (i, 0)) for w in (768, 384, 384)],
        out_specs=pl.BlockSpec((rows, 768), lambda i: (i, 0)),
        out_shape=jax.ShapeDtypeStruct(own.shape, f32),
        compiler_params=pltpu.CompilerParams(vmem_limit_bytes=60 * 2**20),
        cost_estimate=pl.CostEstimate(flops=2**20, bytes_accessed=9 * 2**20, transcendentals=0),
    )(starts, own, head, tail)


def added(terms):
    while len(terms) > 1:
        terms = [x + y for x, y in zip(terms[::2], terms[1::2])]
    return terms[0]


def factor_block(a_ref, m_ref):
    n = PIECE
    row = lax.broadcasted_iota(jnp.int32, (8, n), 0)
    p = a_ref[:8, :]
    q = m_ref[:8, :]
    for lo in range(0, n, 8):
        b = [jnp.broadcast_to(p[:, lo + i : lo + i + 1], (8, n)) for i in range(8)]
        d = jnp.ones((8, n), f32)
        for i in range(8):
            pivot = jnp.broadcast_to(b[i][i : i + 1, :], (8, n))
            d = jnp.where(row == i, pivot, d)
            if i < 7:
                f = jnp.where(row > i, b[i] / pivot, 0.0)
                for j in range(i + 1, 8):
                    b[j] = b[j] - f * jnp.broadcast_to(b[j][i : i + 1, :], (8, n))
                p = p - f * jnp.broadcast_to(p[i : i + 1, :], (8, n))
                q = q - f * jnp.broadcast_to(q[i : i + 1, :], (8, n))
        s = lax.rsqrt(d)
        u = p * s
        v = q * s
        m_ref[lo : lo + 8, :] = v
        at = lo + 8
        if at < n:
            turned = u.T
            cols = [jnp.broadcast_to(turned[at : at + 8, i : i + 1], (8, n)) for i in range(8)]
            p = a_ref[at : at + 8, :] - added([cols[i] * jnp.broadcast_to(u[i : i + 1, :], (8, n)) for i in range(8)])
            q = m_ref[at : at + 8, :] - added([cols[i] * jnp.broadcast_to(v[i : i + 1, :], (8, n)) for i in range(8)])
        if at + 8 < n:
            step = dot(turned, jnp.concatenate([u, v], axis=1), 1, 0)
            a_ref[at + 8 :, :] = a_ref[at + 8 :, :] - step[at + 8 :, :n]
            m_ref[at + 8 :, :] = m_ref[at + 8 :, :] - step[at + 8 :, n:]


def factor_kernel(c_ref, t_ref, a_ref, d_ref, m_ref):
    n = PIECE
    a_ref[...] = c_ref[...]
    t_ref[...] = jnp.zeros((LOCAL, LOCAL), f32)
    eye = lax.broadcasted_iota(jnp.int32, (n, n), 0) == lax.broadcasted_iota(jnp.int32, (n, n), 1)
    for lo in range(0, LOCAL, n):
        hi = lo + n
        d_ref[...] = a_ref[lo:hi, lo:hi]
        m_ref[...] = eye.astype(f32)
        factor_block(d_ref, m_ref)
        m = m_ref[...]
        if lo:
            t_ref[lo:hi, :lo] = dot(m, t_ref[lo:hi, :lo], 1, 0)
        t_ref[lo:hi, lo:hi] = m
        if hi < LOCAL:
            u = dot(m, a_ref[lo:hi, hi:], 1, 0)
            a_ref[hi:, hi:] = a_ref[hi:, hi:] - dot(u, u, 0, 0)
            t_ref[hi:, :hi] = t_ref[hi:, :hi] - dot(u, t_ref[lo:hi, :hi], 0, 0)


def inverse_factor(cov):
    return pl.pallas_call(
        factor_kernel,
        in_specs=[in_vmem],
        out_specs=in_vmem,
        out_shape=jax.ShapeDtypeStruct((LOCAL, LOCAL), f32),
        scratch_shapes=[
            pltpu.VMEM((LOCAL, LOCAL), f32),
            pltpu.VMEM((PIECE, PIECE), f32),
            pltpu.VMEM((PIECE, PIECE), f32),
        ],
        compiler_params=pltpu.CompilerParams(vmem_limit_bytes=16 * 2**20),
        cost_estimate=pl.CostEstimate(flops=36 * 10**9, bytes_accessed=2**21, transcendentals=0),
    )(cov)


def in_order(*arrays):
    return lax.optimization_barrier(arrays)


def body(
    background_realizations,
    realization_expected_data,
    departure_values,
    instrument_dispersion,
    window_piece_offsets,
    window_data_pieces,
    neighbor_piece_ids,
    coupling_indicator,
):
    own_index = lax.axis_index("member")
    region = lax.axis_index("region")
    regions = lax.axis_size("region")
    members = lax.axis_size("member") * background_realizations.shape[0]
    core = lax.rem(region, 2)
    z, y = own_index // COLS, lax.rem(own_index, COLS)
    mine = z * COLS + place_on_row(z, y, core)
    core_word = core.reshape(1)

    rim_s, mid_s = lay_states(core_word, background_realizations)
    rim = exchange(rim_s)

    var = instrument_dispersion.reshape(1, -1)
    to_next, to_last = lay_halo(
        neighbor_piece_ids[0], realization_expected_data, departure_values, var
    )
    before = lax.ppermute(to_next, "region", [(i, (i + 1) % regions) for i in range(regions)])
    behind = lax.ppermute(to_last, "region", [(i, (i - 1) % regions) for i in range(regions)])
    pred_s, innov_s, var_rows = lay_obs(
        jnp.stack([core, mine]),
        window_data_pieces[0],
        realization_expected_data,
        departure_values,
        var,
        before,
        behind,
    )

    def whole(x):
        return x.reshape(members, x.shape[2])

    def in_parts(x):
        return x.reshape(lax.axis_size("member"), -1, x.shape[1])

    cover = jnp.pad(coupling_indicator[0].astype(f32), ((HALF, HALF), (0, 0)))
    cover = lax.dynamic_slice_in_dim(cover, 8 * mine, 14, 0)
    cover = jnp.broadcast_to(cover[:, :, None], (14, OBS_PER, PIECE)).reshape(14, LOCAL)
    starts = lax.dynamic_slice_in_dim(window_piece_offsets[0], mine, 2, 0) - 8 * mine

    def centre(x):
        return x - jnp.mean(x, axis=0, keepdims=True)

    rim, pred_s = in_order(rim, pred_s)
    pred = exchange(pred_s)
    rim = centre(whole(rim))
    head_far = along_snake(rim[:, :384], -1)
    tail_far = along_snake(rim[:, 384:], 1)

    pred, innov_s, rim = in_order(pred, innov_s, rim)
    innov = exchange(innov_s)
    perturbed = centre(whole(pred))
    cov = dot(perturbed, perturbed, 0, 0) / (members - 1.0)
    cov = cov + jnp.eye(LOCAL, dtype=f32) * var_rows[:1]
    root = inverse_factor(cov)

    def gain(x, marks):
        g = lax.dot_general(
            x, perturbed, (((0,), (0,)), ((), ())), precision=high, preferred_element_type=f32
        ) / (members - 1.0)
        return (g.reshape(-1, PIECE, LOCAL) * marks[:, None, :]).reshape(-1, LOCAL)

    root, rim, head_far, tail_far = in_order(root, rim, head_far, tail_far)
    rim_gain = gain(rim, jnp.concatenate([cover[3:6], cover[8:11]]))
    rim_gain, head_far, tail_far = in_order(rim_gain, head_far, tail_far)
    head_gain = gain(head_far, cover[11:])
    tail_gain = gain(tail_far, cover[:3])

    innov, root, mid_s, rim_gain, head_gain, tail_gain = in_order(
        innov, root, mid_s, rim_gain, head_gain, tail_gain
    )
    mid = exchange(mid_s)
    weights = dot(root, dot(root, whole(innov), 1, 1), 0, 0)
    head_inc = dot(weights, head_gain, 0, 1)
    tail_inc = dot(weights, tail_gain, 0, 1)
    head_back = along_snake(head_inc, 1)
    tail_back = along_snake(tail_inc, -1)
    mid, head_inc, tail_inc = in_order(mid, head_inc, tail_inc)
    mid_inc = dot(weights, gain(centre(whole(mid)), cover[6:8]), 0, 1)
    mid_out = exchange(in_parts(mid_inc))
    mid_inc, starts = in_order(mid_inc, starts)
    starts, late_weights = in_order(hold(starts), weights)
    rim_inc = dot(late_weights, rim_gain, 0, 1)
    rim_inc, head_back, tail_back = in_order(rim_inc, head_back, tail_back)
    rim_inc = choose(starts, rim_inc, head_back, tail_back)
    mid_out, rim_inc = in_order(mid_out, rim_inc)
    rim_out = exchange(in_parts(rim_inc))
    return finish(core_word, background_realizations, mid_out, rim_out)


def solution(mesh):
    return jax.shard_map(
        body,
        mesh=mesh,
        in_specs=(
            P("member", "region"),
            P("member", "region"),
            P("member", "region"),
            P("region"),
            P("region", None),
            P("region", None, None),
            P("region", None, None),
            P("region", None, None),
        ),
        out_specs=P("member", "region"),
        check_vma=False,
    )
```

```python
import functools

import jax
import jax.numpy as jnp
from jax import lax
from jax.experimental import pallas as pl
from jax.experimental.pallas import tpu as pltpu
from jax.sharding import PartitionSpec as P

PIECE = 128
OBS_PER = 4
LOCAL = 512
HALF = 3
ROWS, COLS = 8, 4
BOTH = ("member", "region")

highest = lax.Precision.HIGHEST
high = lax.Precision.HIGH
f32 = jnp.float32
in_vmem = pl.BlockSpec(memory_space=pltpu.VMEM)
in_smem = pl.BlockSpec(memory_space=pltpu.SMEM)


def dot(a, b, da, db, precision=highest):
    return lax.dot_general(
        a, b, (((da,), (db,)), ((), ())), precision=precision, preferred_element_type=f32
    )


def column_of(z, r, core):
    return ((r if z % 2 == 0 else COLS - 1 - r) + 2 * core) % COLS


def place_on_row(z, y, core):
    r = lax.rem(y + 2 * core, COLS)
    return jnp.where(lax.rem(z, 2) == 0, r, COLS - 1 - r)


def along_snake(x, step):
    regions = lax.axis_size("region")
    total = ROWS * COLS
    route = []
    for g in range(regions):
        spot = [z * COLS + column_of(z, r, g % 2) for z in range(ROWS) for r in range(COLS)]
        for p in range(total):
            if 0 <= p + step < total:
                route.append((spot[p] * regions + g, spot[p + step] * regions + g))
    return lax.ppermute(x, BOTH, route)


def exchange(x):
    return lax.all_to_all(x, "member", split_axis=0, concat_axis=0, tiled=True)


def states_kernel(core_ref, x_ref, rim_ref, mid_ref):
    z = pl.program_id(0)
    for y in range(COLS):
        base = place_on_row(z, y, core_ref[0]) * 1024
        rim_ref[y, :, :384] = x_ref[:, pl.ds(pl.multiple_of(base, 128), 384)]
        mid_ref[y] = x_ref[:, pl.ds(pl.multiple_of(base + 384, 128), 256)]
        rim_ref[y, :, 384:] = x_ref[:, pl.ds(pl.multiple_of(base + 640, 128), 384)]


def lay_states(core, x):
    members = x.shape[0]
    widths = (768, 256)
    return pl.pallas_call(
        states_kernel,
        grid=(ROWS,),
        in_specs=[in_smem, pl.BlockSpec((members, 4096), lambda z: (0, z))],
        out_specs=[pl.BlockSpec((COLS, members, w), lambda z: (z, 0, 0)) for w in widths],
        out_shape=[jax.ShapeDtypeStruct((ROWS * COLS, members, w), f32) for w in widths],
        compiler_params=pltpu.CompilerParams(vmem_limit_bytes=16 * 2**20),
        cost_estimate=pl.CostEstimate(flops=0, bytes_accessed=2**23, transcendentals=0),
    )(core, x)


def halo_kernel(ids_ref, pred_ref, innov_ref, var_ref, before_ref, after_ref):
    members = pred_ref.shape[0]
    for j, out_ref in enumerate((before_ref, after_ref)):
        for k in range(4):
            at = pl.ds(pl.multiple_of(ids_ref[j, k] * PIECE, PIECE), PIECE)
            to = slice(k * PIECE, (k + 1) * PIECE)
            out_ref[:members, to] = pred_ref[:, at]
            out_ref[members : 2 * members, to] = innov_ref[:, at]
            out_ref[2 * members :, to] = jnp.broadcast_to(var_ref[:, at], (8, PIECE))


def lay_halo(ids, pred, innov, var):
    rows = 2 * pred.shape[0] + 8
    return pl.pallas_call(
        halo_kernel,
        in_specs=[in_smem, in_vmem, in_vmem, in_vmem],
        out_specs=[in_vmem, in_vmem],
        out_shape=[jax.ShapeDtypeStruct((rows, LOCAL), f32)] * 2,
        compiler_params=pltpu.CompilerParams(vmem_limit_bytes=60 * 2**20),
        cost_estimate=pl.CostEstimate(flops=0, bytes_accessed=2**20, transcendentals=0),
    )(ids, pred, innov, var)


def obs_kernel(
    place_ref, lists_ref, pred_ref, innov_ref, var_ref, before_ref, after_ref,
    pred_out, innov_out, var_out, pred_ext, innov_ext, var_ext,
):
    members, own = pred_ref.shape
    for ext, ref, lo, hi in (
        (pred_ext, pred_ref, 0, members),
        (innov_ext, innov_ref, members, 2 * members),
    ):
        ext[:, :own] = ref[...]
        ext[:, own : own + LOCAL] = before_ref[lo:hi, :]
        ext[:, own + LOCAL :] = after_ref[lo:hi, :]
    var_ext[:, :own] = jnp.broadcast_to(var_ref[...], (8, own))
    var_ext[:, own : own + LOCAL] = before_ref[2 * members :, :]
    var_ext[:, own + LOCAL :] = after_ref[2 * members :, :]
    core, mine = place_ref[0], place_ref[1]

    def one(i, carry):
        z, y = i // COLS, lax.rem(i, COLS)
        patch = z * COLS + place_on_row(z, y, core)
        for k in range(OBS_PER):
            at = pl.ds(pl.multiple_of(lists_ref[patch, k] * PIECE, PIECE), PIECE)
            to = slice(k * PIECE, (k + 1) * PIECE)
            pred_out[i, :, to] = pred_ext[:, at]
            innov_out[i, :, to] = innov_ext[:, at]
        return carry

    lax.fori_loop(0, ROWS * COLS, one, 0)
    for k in range(OBS_PER):
        at = pl.ds(pl.multiple_of(lists_ref[mine, k] * PIECE, PIECE), PIECE)
        var_out[:, k * PIECE : (k + 1) * PIECE] = var_ext[:, at]


def lay_obs(place, lists, pred, innov, var, before, after):
    members, own = pred.shape
    sent = jax.ShapeDtypeStruct((ROWS * COLS, members, LOCAL), f32)
    return pl.pallas_call(
        obs_kernel,
        in_specs=[in_smem, in_smem] + [in_vmem] * 5,
        out_specs=[in_vmem] * 3,
        out_shape=[sent, sent, jax.ShapeDtypeStruct((8, LOCAL), f32)],
        scratch_shapes=[
            pltpu.VMEM((members, own + 2 * LOCAL), f32),
            pltpu.VMEM((members, own + 2 * LOCAL), f32),
            pltpu.VMEM((8, own + 2 * LOCAL), f32),
        ],
        compiler_params=pltpu.CompilerParams(vmem_limit_bytes=60 * 2**20),
        cost_estimate=pl.CostEstimate(flops=0, bytes_accessed=6 * 2**20, transcendentals=0),
    )(place, lists, pred, innov, var, before, after)


def finish_kernel(core_ref, x_ref, mid_ref, rim_ref, out_ref):
    z = pl.program_id(0)
    for y in range(COLS):
        base = place_on_row(z, y, core_ref[0]) * 1024
        for lo, width, ref, at in ((0, 384, rim_ref, 0), (384, 256, mid_ref, 0), (640, 384, rim_ref, 384)):
            to = pl.ds(pl.multiple_of(base + lo, 128), width)
            out_ref[:, to] = x_ref[:, to] + ref[y, :, at : at + width]


def finish(core, x, mid, rim):
    members = x.shape[0]
    return pl.pallas_call(
        finish_kernel,
        grid=(ROWS,),
        in_specs=[
            in_smem,
            pl.BlockSpec((members, 4096), lambda z: (0, z)),
            pl.BlockSpec((COLS, members, 256), lambda z: (z, 0, 0)),
            pl.BlockSpec((COLS, members, 768), lambda z: (z, 0, 0)),
        ],
        out_specs=pl.BlockSpec((members, 4096), lambda z: (0, z)),
        out_shape=jax.ShapeDtypeStruct(x.shape, f32),
        compiler_params=pltpu.CompilerParams(vmem_limit_bytes=16 * 2**20),
        cost_estimate=pl.CostEstimate(flops=2**20, bytes_accessed=3 * 2**22, transcendentals=0),
    )(core, x, mid, rim)


def hold_kernel(in_ref, out_ref):
    out_ref[0] = in_ref[0]
    out_ref[1] = in_ref[1]


def hold(starts):
    return pl.pallas_call(
        hold_kernel,
        in_specs=[in_smem],
        out_specs=in_smem,
        out_shape=jax.ShapeDtypeStruct((2,), jnp.int32),
        cost_estimate=pl.CostEstimate(flops=10**11, bytes_accessed=8, transcendentals=0),
    )(starts)


def choose_kernel(side, starts_ref, own_ref, back_ref, out_ref):
    for j in range(HALF):
        at = slice(j * PIECE, (j + 1) * PIECE)
        theirs = j < starts_ref[0] if side == 0 else j + 5 >= starts_ref[1]
        out_ref[:, at] = jnp.where(theirs, back_ref[:, at], own_ref[:, at])


def choose(side, starts, own, back):
    rows, width = own.shape[0] // 2, HALF * PIECE
    return pl.pallas_call(
        functools.partial(choose_kernel, side),
        grid=(2,),
        in_specs=[
            in_smem,
            pl.BlockSpec((rows, width), lambda i: (i, side)),
            pl.BlockSpec((rows, width), lambda i: (i, 0)),
        ],
        out_specs=pl.BlockSpec((rows, width), lambda i: (i, side)),
        out_shape=jax.ShapeDtypeStruct(own.shape, f32),
        input_output_aliases={1: 0},
        compiler_params=pltpu.CompilerParams(vmem_limit_bytes=60 * 2**20),
        cost_estimate=pl.CostEstimate(flops=2**20, bytes_accessed=5 * 2**20, transcendentals=0),
    )(starts, own, back)


def added(terms):
    while len(terms) > 1:
        terms = [x + y for x, y in zip(terms[::2], terms[1::2])]
    return terms[0]


def factor_block(a_ref, m_ref):
    n = PIECE
    row = lax.broadcasted_iota(jnp.int32, (8, n), 0)
    p = a_ref[:8, :]
    q = m_ref[:8, :]
    for lo in range(0, n, 8):
        b = [jnp.broadcast_to(p[:, lo + i : lo + i + 1], (8, n)) for i in range(8)]
        d = jnp.ones((8, n), f32)
        for i in range(8):
            pivot = jnp.broadcast_to(b[i][i : i + 1, :], (8, n))
            d = jnp.where(row == i, pivot, d)
            if i < 7:
                f = jnp.where(row > i, b[i] / pivot, 0.0)
                for j in range(i + 1, 8):
                    b[j] = b[j] - f * jnp.broadcast_to(b[j][i : i + 1, :], (8, n))
                p = p - f * jnp.broadcast_to(p[i : i + 1, :], (8, n))
                q = q - f * jnp.broadcast_to(q[i : i + 1, :], (8, n))
        s = lax.rsqrt(d)
        u = p * s
        v = q * s
        m_ref[lo : lo + 8, :] = v
        at = lo + 8
        if at < n:
            turned = u.T
            cols = [jnp.broadcast_to(turned[at : at + 8, i : i + 1], (8, n)) for i in range(8)]
            p = a_ref[at : at + 8, :] - added([cols[i] * jnp.broadcast_to(u[i : i + 1, :], (8, n)) for i in range(8)])
            q = m_ref[at : at + 8, :] - added([cols[i] * jnp.broadcast_to(v[i : i + 1, :], (8, n)) for i in range(8)])
        if at + 8 < n:
            step = dot(turned, jnp.concatenate([u, v], axis=1), 1, 0)
            a_ref[at + 8 :, :] = a_ref[at + 8 :, :] - step[at + 8 :, :n]
            m_ref[at + 8 :, :] = m_ref[at + 8 :, :] - step[at + 8 :, n:]


def factor_kernel(c_ref, t_ref, a_ref, d_ref, m_ref):
    n = PIECE
    a_ref[...] = c_ref[...]
    t_ref[...] = jnp.zeros((LOCAL, LOCAL), f32)
    eye = lax.broadcasted_iota(jnp.int32, (n, n), 0) == lax.broadcasted_iota(jnp.int32, (n, n), 1)
    for lo in range(0, LOCAL, n):
        hi = lo + n
        d_ref[...] = a_ref[lo:hi, lo:hi]
        m_ref[...] = eye.astype(f32)
        factor_block(d_ref, m_ref)
        m = m_ref[...]
        if lo:
            t_ref[lo:hi, :lo] = dot(m, t_ref[lo:hi, :lo], 1, 0)
        t_ref[lo:hi, lo:hi] = m
        if hi < LOCAL:
            u = dot(m, a_ref[lo:hi, hi:], 1, 0)
            a_ref[hi:, hi:] = a_ref[hi:, hi:] - dot(u, u, 0, 0)
            t_ref[hi:, :hi] = t_ref[hi:, :hi] - dot(u, t_ref[lo:hi, :hi], 0, 0)


def inverse_factor(cov):
    return pl.pallas_call(
        factor_kernel,
        in_specs=[in_vmem],
        out_specs=in_vmem,
        out_shape=jax.ShapeDtypeStruct((LOCAL, LOCAL), f32),
        scratch_shapes=[
            pltpu.VMEM((LOCAL, LOCAL), f32),
            pltpu.VMEM((PIECE, PIECE), f32),
            pltpu.VMEM((PIECE, PIECE), f32),
        ],
        compiler_params=pltpu.CompilerParams(vmem_limit_bytes=16 * 2**20),
        cost_estimate=pl.CostEstimate(flops=36 * 10**9, bytes_accessed=2**21, transcendentals=0),
    )(cov)


def in_order(*arrays):
    return lax.optimization_barrier(arrays)


def body(
    background_realizations,
    realization_expected_data,
    departure_values,
    instrument_dispersion,
    window_piece_offsets,
    window_data_pieces,
    neighbor_piece_ids,
    coupling_indicator,
):
    own_index = lax.axis_index("member")
    region = lax.axis_index("region")
    regions = lax.axis_size("region")
    members = lax.axis_size("member") * background_realizations.shape[0]
    core = lax.rem(region, 2)
    z, y = own_index // COLS, lax.rem(own_index, COLS)
    mine = z * COLS + place_on_row(z, y, core)
    core_word = core.reshape(1)

    rim_s, mid_s = lay_states(core_word, background_realizations)
    rim = exchange(rim_s)

    var = instrument_dispersion.reshape(1, -1)
    to_next, to_last = lay_halo(
        neighbor_piece_ids[0], realization_expected_data, departure_values, var
    )
    before = lax.ppermute(to_next, "region", [(i, (i + 1) % regions) for i in range(regions)])
    behind = lax.ppermute(to_last, "region", [(i, (i - 1) % regions) for i in range(regions)])
    pred_s, innov_s, var_rows = lay_obs(
        jnp.stack([core, mine]),
        window_data_pieces[0],
        realization_expected_data,
        departure_values,
        var,
        before,
        behind,
    )

    def whole(x):
        return x.reshape(members, x.shape[2])

    def in_parts(x):
        return x.reshape(lax.axis_size("member"), -1, x.shape[1])

    cover = jnp.pad(coupling_indicator[0].astype(f32), ((HALF, HALF), (0, 0)))
    cover = lax.dynamic_slice_in_dim(cover, 8 * mine, 14, 0)
    cover = jnp.broadcast_to(cover[:, :, None], (14, OBS_PER, PIECE)).reshape(14, LOCAL)
    starts = lax.dynamic_slice_in_dim(window_piece_offsets[0], mine, 2, 0) - 8 * mine

    def centre(x):
        return x - jnp.mean(x, axis=0, keepdims=True)

    rim, pred_s = in_order(rim, pred_s)
    pred = exchange(pred_s)
    rim = centre(whole(rim))
    head_far = along_snake(rim[:, :384], -1)
    tail_far = along_snake(rim[:, 384:], 1)

    pred, innov_s, rim = in_order(pred, innov_s, rim)
    innov = exchange(innov_s)
    perturbed = centre(whole(pred))
    cov = dot(perturbed, perturbed, 0, 0) / (members - 1.0)
    cov = cov + jnp.eye(LOCAL, dtype=f32) * var_rows[:1]
    root = inverse_factor(cov)

    def gain(x, marks):
        g = dot(x, perturbed, 0, 0, high) / (members - 1.0)
        return (g.reshape(-1, PIECE, LOCAL) * marks[:, None, :]).reshape(-1, LOCAL)

    def solved(g):
        return dot(root, dot(root, g, 1, 1), 0, 0)

    root, rim, head_far, tail_far = in_order(root, rim, head_far, tail_far)
    rim_gain = gain(rim, jnp.concatenate([cover[3:6], cover[8:11]]))
    rim_gain, head_far, tail_far = in_order(rim_gain, head_far, tail_far)
    head_solved = solved(gain(head_far, cover[11:]))
    tail_solved = solved(gain(tail_far, cover[:3]))

    innov, root, mid_s, rim_gain, head_solved, tail_solved = in_order(
        innov, root, mid_s, rim_gain, head_solved, tail_solved
    )
    mid = exchange(mid_s)
    innov = whole(innov)
    head_inc = dot(innov, head_solved, 1, 0, high)
    tail_inc = dot(innov, tail_solved, 1, 0, high)
    head_back = along_snake(head_inc, 1)
    tail_back = along_snake(tail_inc, -1)
    innov, head_inc, tail_inc = in_order(innov, head_inc, tail_inc)
    weights = dot(root, dot(root, innov, 1, 1), 0, 0)
    mid, weights = in_order(mid, weights)
    mid_inc = dot(weights, gain(centre(whole(mid)), cover[6:8]), 0, 1)
    mid_out = exchange(in_parts(mid_inc))
    mid_inc, starts = in_order(mid_inc, starts)
    starts, late_weights = in_order(hold(starts), weights)
    rim_inc = dot(late_weights, rim_gain, 0, 1)
    rim_inc, head_back = in_order(rim_inc, head_back)
    rim_inc = choose(0, starts, rim_inc, head_back)
    rim_inc, tail_back = in_order(rim_inc, tail_back)
    rim_inc = choose(1, starts, rim_inc, tail_back)
    mid_out, rim_inc = in_order(mid_out, rim_inc)
    rim_out = exchange(in_parts(rim_inc))
    return finish(core_word, background_realizations, mid_out, rim_out)


def solution(mesh):
    return jax.shard_map(
        body,
        mesh=mesh,
        in_specs=(
            P("member", "region"),
            P("member", "region"),
            P("member", "region"),
            P("region"),
            P("region", None),
            P("region", None, None),
            P("region", None, None),
            P("region", None, None),
        ),
        out_specs=P("member", "region"),
        check_vma=False,
    )
```

```python
import functools

import jax
import jax.numpy as jnp
from jax import lax
from jax.experimental import pallas as pl
from jax.experimental.pallas import tpu as pltpu
from jax.sharding import PartitionSpec as P

PIECE = 128
OBS_PER = 4
LOCAL = 512
HALF = 3
ROWS, COLS = 8, 4
BOTH = ("member", "region")

highest = lax.Precision.HIGHEST
high = lax.Precision.HIGH
f32 = jnp.float32
in_vmem = pl.BlockSpec(memory_space=pltpu.VMEM)
in_smem = pl.BlockSpec(memory_space=pltpu.SMEM)


def dot(a, b, da, db, precision=highest):
    return lax.dot_general(
        a, b, (((da,), (db,)), ((), ())), precision=precision, preferred_element_type=f32
    )


def column_of(z, r, core):
    return ((r if z % 2 == 0 else COLS - 1 - r) + 2 * core) % COLS


def place_on_row(z, y, core):
    r = lax.rem(y + 2 * core, COLS)
    return jnp.where(lax.rem(z, 2) == 0, r, COLS - 1 - r)


def along_snake(x, step):
    regions = lax.axis_size("region")
    total = ROWS * COLS
    route = []
    for g in range(regions):
        spot = [z * COLS + column_of(z, r, g % 2) for z in range(ROWS) for r in range(COLS)]
        for p in range(total):
            if 0 <= p + step < total:
                route.append((spot[p] * regions + g, spot[p + step] * regions + g))
    return lax.ppermute(x, BOTH, route)


def exchange(x):
    return lax.all_to_all(x, "member", split_axis=0, concat_axis=0, tiled=True)


def states_kernel(core_ref, x_ref, rim_ref, mid_ref, sems):
    copies = []
    for z in range(ROWS):
        for y in range(COLS):
            base = (z * COLS + place_on_row(z, y, core_ref[0])) * 1024
            i = z * COLS + y
            for k, (lo, width, ref, at) in enumerate(
                ((0, 384, rim_ref, 0), (640, 384, rim_ref, 384), (384, 256, mid_ref, 0))
            ):
                copies.append(
                    pltpu.make_async_copy(
                        x_ref.at[:, pl.ds(pl.multiple_of(base + lo, 128), width)],
                        ref.at[i, :, pl.ds(at, width)],
                        sems.at[i, k],
                    )
                )
                copies[-1].start()
    for copy in copies:
        copy.wait()


def lay_states(core, x):
    members = x.shape[0]
    return pl.pallas_call(
        states_kernel,
        in_specs=[in_smem, in_vmem],
        out_specs=[pl.BlockSpec(memory_space=pl.ANY)] * 2,
        out_shape=[jax.ShapeDtypeStruct((ROWS * COLS, members, w), f32) for w in (768, 256)],
        scratch_shapes=[pltpu.SemaphoreType.DMA((ROWS * COLS, 3))],
        compiler_params=pltpu.CompilerParams(vmem_limit_bytes=16 * 2**20),
        cost_estimate=pl.CostEstimate(flops=0, bytes_accessed=2**23, transcendentals=0),
    )(core, x)


def halo_kernel(ids_ref, pred_ref, innov_ref, var_ref, before_ref, after_ref):
    members = pred_ref.shape[0]
    for j, out_ref in enumerate((before_ref, after_ref)):
        for k in range(4):
            at = pl.ds(pl.multiple_of(ids_ref[j, k] * PIECE, PIECE), PIECE)
            to = slice(k * PIECE, (k + 1) * PIECE)
            out_ref[:members, to] = pred_ref[:, at]
            out_ref[members : 2 * members, to] = innov_ref[:, at]
            out_ref[2 * members :, to] = jnp.broadcast_to(var_ref[:, at], (8, PIECE))


def lay_halo(ids, pred, innov, var):
    rows = 2 * pred.shape[0] + 8
    return pl.pallas_call(
        halo_kernel,
        in_specs=[in_smem, in_vmem, in_vmem, in_vmem],
        out_specs=[in_vmem, in_vmem],
        out_shape=[jax.ShapeDtypeStruct((rows, LOCAL), f32)] * 2,
        compiler_params=pltpu.CompilerParams(vmem_limit_bytes=60 * 2**20),
        cost_estimate=pl.CostEstimate(flops=0, bytes_accessed=2**20, transcendentals=0),
    )(ids, pred, innov, var)


def obs_kernel(
    place_ref, lists_ref, pred_ref, innov_ref, var_ref, before_ref, after_ref,
    pred_out, innov_out, var_out, pred_ext, innov_ext, var_ext,
):
    members, own = pred_ref.shape
    for ext, ref, lo, hi in (
        (pred_ext, pred_ref, 0, members),
        (innov_ext, innov_ref, members, 2 * members),
    ):
        ext[:, :own] = ref[...]
        ext[:, own : own + LOCAL] = before_ref[lo:hi, :]
        ext[:, own + LOCAL :] = after_ref[lo:hi, :]
    var_ext[:, :own] = jnp.broadcast_to(var_ref[...], (8, own))
    var_ext[:, own : own + LOCAL] = before_ref[2 * members :, :]
    var_ext[:, own + LOCAL :] = after_ref[2 * members :, :]
    core, mine = place_ref[0], place_ref[1]

    def one(i, carry):
        z, y = i // COLS, lax.rem(i, COLS)
        patch = z * COLS + place_on_row(z, y, core)
        for k in range(OBS_PER):
            at = pl.ds(pl.multiple_of(lists_ref[patch, k] * PIECE, PIECE), PIECE)
            to = slice(k * PIECE, (k + 1) * PIECE)
            pred_out[i, :, to] = pred_ext[:, at]
            innov_out[i, :, to] = innov_ext[:, at]
        return carry

    lax.fori_loop(0, ROWS * COLS, one, 0)
    for k in range(OBS_PER):
        at = pl.ds(pl.multiple_of(lists_ref[mine, k] * PIECE, PIECE), PIECE)
        var_out[:, k * PIECE : (k + 1) * PIECE] = var_ext[:, at]


def lay_obs(place, lists, pred, innov, var, before, after):
    members, own = pred.shape
    sent = jax.ShapeDtypeStruct((ROWS * COLS, members, LOCAL), f32)
    return pl.pallas_call(
        obs_kernel,
        in_specs=[in_smem, in_smem] + [in_vmem] * 5,
        out_specs=[in_vmem] * 3,
        out_shape=[sent, sent, jax.ShapeDtypeStruct((8, LOCAL), f32)],
        scratch_shapes=[
            pltpu.VMEM((members, own + 2 * LOCAL), f32),
            pltpu.VMEM((members, own + 2 * LOCAL), f32),
            pltpu.VMEM((8, own + 2 * LOCAL), f32),
        ],
        compiler_params=pltpu.CompilerParams(vmem_limit_bytes=60 * 2**20),
        cost_estimate=pl.CostEstimate(flops=0, bytes_accessed=6 * 2**20, transcendentals=0),
    )(place, lists, pred, innov, var, before, after)


def finish_kernel(core_ref, x_ref, mid_ref, rim_ref, out_ref):
    z = pl.program_id(0)
    for y in range(COLS):
        base = place_on_row(z, y, core_ref[0]) * 1024
        for lo, width, ref, at in ((0, 384, rim_ref, 0), (384, 256, mid_ref, 0), (640, 384, rim_ref, 384)):
            to = pl.ds(pl.multiple_of(base + lo, 128), width)
            out_ref[:, to] = x_ref[:, to] + ref[y, :, at : at + width]


def finish(core, x, mid, rim):
    members = x.shape[0]
    return pl.pallas_call(
        finish_kernel,
        grid=(ROWS,),
        in_specs=[
            in_smem,
            pl.BlockSpec((members, 4096), lambda z: (0, z)),
            pl.BlockSpec((COLS, members, 256), lambda z: (z, 0, 0)),
            pl.BlockSpec((COLS, members, 768), lambda z: (z, 0, 0)),
        ],
        out_specs=pl.BlockSpec((members, 4096), lambda z: (0, z)),
        out_shape=jax.ShapeDtypeStruct(x.shape, f32),
        compiler_params=pltpu.CompilerParams(vmem_limit_bytes=16 * 2**20),
        cost_estimate=pl.CostEstimate(flops=2**20, bytes_accessed=3 * 2**22, transcendentals=0),
    )(core, x, mid, rim)


def hold_kernel(in_ref, out_ref):
    out_ref[0] = in_ref[0]
    out_ref[1] = in_ref[1]


def hold(starts):
    return pl.pallas_call(
        hold_kernel,
        in_specs=[in_smem],
        out_specs=in_smem,
        out_shape=jax.ShapeDtypeStruct((2,), jnp.int32),
        cost_estimate=pl.CostEstimate(flops=10**11, bytes_accessed=8, transcendentals=0),
    )(starts)


def choose_kernel(side, starts_ref, own_ref, back_ref, out_ref):
    for j in range(HALF):
        at = slice(j * PIECE, (j + 1) * PIECE)
        theirs = j < starts_ref[0] if side == 0 else j + 5 >= starts_ref[1]
        out_ref[:, at] = jnp.where(theirs, back_ref[:, at], own_ref[:, at])


def choose(side, starts, own, back):
    rows, width = own.shape[0] // 2, HALF * PIECE
    return pl.pallas_call(
        functools.partial(choose_kernel, side),
        grid=(2,),
        in_specs=[
            in_smem,
            pl.BlockSpec((rows, width), lambda i: (i, side)),
            pl.BlockSpec((rows, width), lambda i: (i, 0)),
        ],
        out_specs=pl.BlockSpec((rows, width), lambda i: (i, side)),
        out_shape=jax.ShapeDtypeStruct(own.shape, f32),
        input_output_aliases={1: 0},
        compiler_params=pltpu.CompilerParams(vmem_limit_bytes=60 * 2**20),
        cost_estimate=pl.CostEstimate(flops=2**20, bytes_accessed=5 * 2**20, transcendentals=0),
    )(starts, own, back)


def added(terms):
    while len(terms) > 1:
        terms = [x + y for x, y in zip(terms[::2], terms[1::2])]
    return terms[0]


def factor_block(a_ref, m_ref):
    n = PIECE
    row = lax.broadcasted_iota(jnp.int32, (8, n), 0)
    p = a_ref[:8, :]
    q = m_ref[:8, :]
    for lo in range(0, n, 8):
        b = [jnp.broadcast_to(p[:, lo + i : lo + i + 1], (8, n)) for i in range(8)]
        d = jnp.ones((8, n), f32)
        for i in range(8):
            pivot = jnp.broadcast_to(b[i][i : i + 1, :], (8, n))
            d = jnp.where(row == i, pivot, d)
            if i < 7:
                f = jnp.where(row > i, b[i] / pivot, 0.0)
                for j in range(i + 1, 8):
                    b[j] = b[j] - f * jnp.broadcast_to(b[j][i : i + 1, :], (8, n))
                p = p - f * jnp.broadcast_to(p[i : i + 1, :], (8, n))
                q = q - f * jnp.broadcast_to(q[i : i + 1, :], (8, n))
        s = lax.rsqrt(d)
        u = p * s
        v = q * s
        m_ref[lo : lo + 8, :] = v
        at = lo + 8
        if at < n:
            turned = u.T
            cols = [jnp.broadcast_to(turned[at : at + 8, i : i + 1], (8, n)) for i in range(8)]
            p = a_ref[at : at + 8, :] - added([cols[i] * jnp.broadcast_to(u[i : i + 1, :], (8, n)) for i in range(8)])
            q = m_ref[at : at + 8, :] - added([cols[i] * jnp.broadcast_to(v[i : i + 1, :], (8, n)) for i in range(8)])
        if at + 8 < n:
            step = dot(turned, jnp.concatenate([u, v], axis=1), 1, 0)
            a_ref[at + 8 :, :] = a_ref[at + 8 :, :] - step[at + 8 :, :n]
            m_ref[at + 8 :, :] = m_ref[at + 8 :, :] - step[at + 8 :, n:]


def factor_kernel(c_ref, t_ref, a_ref, d_ref, m_ref):
    n = PIECE
    a_ref[...] = c_ref[...]
    t_ref[...] = jnp.zeros((LOCAL, LOCAL), f32)
    eye = lax.broadcasted_iota(jnp.int32, (n, n), 0) == lax.broadcasted_iota(jnp.int32, (n, n), 1)
    for lo in range(0, LOCAL, n):
        hi = lo + n
        d_ref[...] = a_ref[lo:hi, lo:hi]
        m_ref[...] = eye.astype(f32)
        factor_block(d_ref, m_ref)
        m = m_ref[...]
        if lo:
            t_ref[lo:hi, :lo] = dot(m, t_ref[lo:hi, :lo], 1, 0)
        t_ref[lo:hi, lo:hi] = m
        if hi < LOCAL:
            u = dot(m, a_ref[lo:hi, hi:], 1, 0)
            a_ref[hi:, hi:] = a_ref[hi:, hi:] - dot(u, u, 0, 0)
            t_ref[hi:, :hi] = t_ref[hi:, :hi] - dot(u, t_ref[lo:hi, :hi], 0, 0)


def inverse_factor(cov):
    return pl.pallas_call(
        factor_kernel,
        in_specs=[in_vmem],
        out_specs=in_vmem,
        out_shape=jax.ShapeDtypeStruct((LOCAL, LOCAL), f32),
        scratch_shapes=[
            pltpu.VMEM((LOCAL, LOCAL), f32),
            pltpu.VMEM((PIECE, PIECE), f32),
            pltpu.VMEM((PIECE, PIECE), f32),
        ],
        compiler_params=pltpu.CompilerParams(vmem_limit_bytes=16 * 2**20),
        cost_estimate=pl.CostEstimate(flops=2 * 10**11, bytes_accessed=2**21, transcendentals=0),
    )(cov)


def in_order(*arrays):
    return lax.optimization_barrier(arrays)


def body(
    background_realizations,
    realization_expected_data,
    departure_values,
    instrument_dispersion,
    window_piece_offsets,
    window_data_pieces,
    neighbor_piece_ids,
    coupling_indicator,
):
    own_index = lax.axis_index("member")
    region = lax.axis_index("region")
    regions = lax.axis_size("region")
    members = lax.axis_size("member") * background_realizations.shape[0]
    core = lax.rem(region, 2)
    z, y = own_index // COLS, lax.rem(own_index, COLS)
    mine = z * COLS + place_on_row(z, y, core)
    core_word = core.reshape(1)

    rim_s, mid_s = lay_states(core_word, background_realizations)
    rim = exchange(rim_s)

    var = instrument_dispersion.reshape(1, -1)
    to_next, to_last = lay_halo(
        neighbor_piece_ids[0], realization_expected_data, departure_values, var
    )
    before = lax.ppermute(to_next, "region", [(i, (i + 1) % regions) for i in range(regions)])
    behind = lax.ppermute(to_last, "region", [(i, (i - 1) % regions) for i in range(regions)])
    pred_s, innov_s, var_rows = lay_obs(
        jnp.stack([core, mine]),
        window_data_pieces[0],
        realization_expected_data,
        departure_values,
        var,
        before,
        behind,
    )

    def whole(x):
        return x.reshape(members, x.shape[2])

    def in_parts(x):
        return x.reshape(lax.axis_size("member"), -1, x.shape[1])

    cover = jnp.pad(coupling_indicator[0].astype(f32), ((HALF, HALF), (0, 0)))
    cover = lax.dynamic_slice_in_dim(cover, 8 * mine, 14, 0)
    cover = jnp.broadcast_to(cover[:, :, None], (14, OBS_PER, PIECE)).reshape(14, LOCAL)
    starts = lax.dynamic_slice_in_dim(window_piece_offsets[0], mine, 2, 0) - 8 * mine

    def centre(x):
        return x - jnp.mean(x, axis=0, keepdims=True)

    rim, pred_s = in_order(rim, pred_s)
    pred = exchange(pred_s)
    rim = centre(whole(rim))
    head_far = along_snake(rim[:, :384], -1)
    tail_far = along_snake(rim[:, 384:], 1)

    pred, innov_s, rim = in_order(pred, innov_s, rim)
    innov = exchange(innov_s)
    perturbed = centre(whole(pred))
    cov = dot(perturbed, perturbed, 0, 0) / (members - 1.0)
    cov = cov + jnp.eye(LOCAL, dtype=f32) * var_rows[:1]
    root = inverse_factor(cov)

    def gain(x, marks):
        g = dot(x, perturbed, 0, 0, high) / (members - 1.0)
        return (g.reshape(-1, PIECE, LOCAL) * marks[:, None, :]).reshape(-1, LOCAL)

    def solved(g):
        return dot(root, dot(root, g, 1, 1), 0, 0)

    root, head_far, tail_far = in_order(root, head_far, tail_far)
    head_solved = solved(gain(head_far, cover[11:]))
    tail_solved = solved(gain(tail_far, cover[:3]))

    innov, root, mid_s, head_solved, tail_solved = in_order(
        innov, root, mid_s, head_solved, tail_solved
    )
    mid = exchange(mid_s)
    innov = whole(innov)
    head_inc = dot(innov, head_solved, 1, 0, high)
    tail_inc = dot(innov, tail_solved, 1, 0, high)
    head_back = along_snake(head_inc, 1)
    tail_back = along_snake(tail_inc, -1)
    innov, head_inc, tail_inc = in_order(innov, head_inc, tail_inc)
    weights = dot(root, dot(root, innov, 1, 1), 0, 0)
    mid, weights = in_order(mid, weights)
    mid_inc = dot(weights, gain(centre(whole(mid)), cover[6:8]), 0, 1)
    mid_out = exchange(in_parts(mid_inc))
    mid_inc, starts = in_order(mid_inc, starts)
    starts, late_weights, rim = in_order(hold(starts), weights, rim)
    rim_gain = gain(rim, jnp.concatenate([cover[3:6], cover[8:11]]))
    rim_inc = dot(late_weights, rim_gain, 0, 1)
    rim_inc, head_back = in_order(rim_inc, head_back)
    rim_inc = choose(0, starts, rim_inc, head_back)
    rim_inc, tail_back = in_order(rim_inc, tail_back)
    rim_inc = choose(1, starts, rim_inc, tail_back)
    mid_out, rim_inc = in_order(mid_out, rim_inc)
    rim_out = exchange(in_parts(rim_inc))
    return finish(core_word, background_realizations, mid_out, rim_out)


def solution(mesh):
    return jax.shard_map(
        body,
        mesh=mesh,
        in_specs=(
            P("member", "region"),
            P("member", "region"),
            P("member", "region"),
            P("region"),
            P("region", None),
            P("region", None, None),
            P("region", None, None),
            P("region", None, None),
        ),
        out_specs=P("member", "region"),
        check_vma=False,
    )
```
